256 devices in a mesh: px: 4 (over z_hi), py: 8 (over y, core), mz: 8 (over z_lo, x).
Axes of the slice: x: 4, y: 4, z: 8 (z_hi: 4, z_lo: 2; z = z_hi * 2 + z_lo), core: 2. Of those that a mesh axis runs over, the one named last changes fastest.
Arguments:
- tensor: float32 [512, 1024, 1024], P('px', 'py', 'mz'), may hold values from 0 to 1573632, as said below
- factor_a: float32 [512, 256], P('px'), may hold values from 0 to 1
- factor_b: float32 [1024, 256], P('py'), may hold values from 0 to 1
- factor_c: float32 [1024, 256], P('mz'), may hold values from 0 to 1
Outputs:
- new_a: float32 [512, 256], P('px')
- new_b: float32 [1024, 256], P('py')
- new_c: float32 [1024, 256], P('mz')
The draws below stay inside these ranges and needn't reach their ends.
Inputs may be any that keep to these rules, and one draw needn't show every extreme that they name: `tensor`: nonnegative intensities.
All inputs are finite; a program needn't handle non-finite values.
Results may differ from the reference program's by a relative error of at most 0.00015.
Values sent between devices are 32-bit elements; how exact they have to be, the bound alone decides.
No kernel may reach another device: no remote copies, remote signals or barrier semaphores. Data moves between devices by JAX's collectives and lax.ppermute only.
A program may use at most 128 MiB of HBM per device.

```python
import jax
import jax.numpy as jnp
from jax import lax

RANK = 256
PASSES = 2
NX = 512
NY = 1024
NZ = 1024


def log_spread(key, shape, lower_end, upper_end):
    return jnp.exp(jax.random.uniform(key, shape, jnp.float32, jnp.log(lower_end), jnp.log(upper_end)))


def draw_tensor(key, part):
    key = jax.random.fold_in(key, 11)
    key_x, key_y, key_amp, key_peak, key_height, key_cell = jax.random.split(key, 6)
    lower_end, upper_end = (0.5, 2.0)
    amp_low, amp_high = (0.3, 3.0)
    height_top = 10.0
    cell_noise = log_spread(key_cell, (NX, NY, NZ), 0.5, 2.0)
    along_x = log_spread(key_x, (NX, 1, 1), lower_end, upper_end)
    along_y = log_spread(key_y, (1, NY, 1), lower_end, upper_end)
    region_amp = log_spread(key_amp, (64, 1), amp_low, amp_high)
    peak_mask = jax.random.bernoulli(key_peak, min(1.0, 8.0 / NZ), (64, NZ)).astype(jnp.float32)
    heights = log_spread(key_height, (64, NZ), 1.0, height_top) * (NZ / 32.0)
    spectra = region_amp * (0.25 + peak_mask * heights)
    row_region = jnp.arange(NX, dtype=jnp.int32) * 8 // NX
    col_region = jnp.arange(NY, dtype=jnp.int32) * 8 // NY
    region_index = row_region[:, None] * 8 + col_region[None, :]
    profile = jnp.take(spectra, region_index, axis=0)
    return 0.1 * RANK * along_x * along_y * profile * cell_noise


def block_levels(key, dims, pieces, low, top_value):
    loudness, own = 1.0, jax.random.fold_in(key, 6)
    for axis_at, parts in pieces:
        steps = jnp.exp(jax.random.uniform(jax.random.fold_in(own, axis_at), (parts,), jnp.float32, low / len(pieces), top_value / len(pieces)))
        loudness = loudness * jnp.repeat(steps, dims[axis_at] // parts).reshape([-1 if axis == axis_at else 1 for axis in range(len(dims))])
    return loudness


def setup_inputs(seed: int = 0) -> dict:
    streams_of = jax.random.split(jax.random.key(seed), 5)
    tensor = draw_tensor(jax.random.fold_in(streams_of[4], 71), 0)
    factor_a = jnp.clip(1.0 * jax.random.uniform(streams_of[1], (NX, RANK), jnp.float32) ** block_levels(streams_of[1], (NX, RANK), ((0, 4),), -0.2, 0.2), 0.0, 1.0)
    factor_b = jnp.clip(1.0 * jax.random.uniform(streams_of[2], (NY, RANK), jnp.float32) ** block_levels(streams_of[2], (NY, RANK), ((0, 8),), -0.2, 0.2), 0.0, 1.0)
    factor_c = jnp.clip(1.0 * jax.random.uniform(streams_of[3], (NZ, RANK), jnp.float32) ** block_levels(streams_of[3], (NZ, RANK), ((0, 8),), -0.2, 0.2), 0.0, 1.0)
    return dict(tensor=tensor, factor_a=factor_a, factor_b=factor_b, factor_c=factor_c)


exact_mode = lax.Precision.HIGHEST


def gram_of(factor):
    return jnp.dot(factor.T, factor, precision=exact_mode, preferred_element_type=jnp.float32)


def update_factor(factor, mttkrp, gram_mix):
    scale_cols = jnp.sum(gram_mix, axis=0) + 1.0
    for sweep_pass in range(PASSES):
        product = jnp.dot(factor, gram_mix, precision=exact_mode, preferred_element_type=jnp.float32)
        factor = jnp.maximum(factor + (mttkrp - product) / scale_cols, 0.0)
    return factor


def reference(tensor, factor_a, factor_b, factor_c):
    gram_b = gram_of(factor_b)
    gram_c = gram_of(factor_c)
    partial_c = jnp.dot(tensor.reshape(NX * NY, NZ), factor_c, precision=exact_mode, preferred_element_type=jnp.float32)
    mttkrp_a = jnp.einsum("ijr,jr->ir", partial_c.reshape(NX, NY, RANK), factor_b, precision=exact_mode, preferred_element_type=jnp.float32)
    new_a = update_factor(factor_a, mttkrp_a, gram_b * gram_c)
    gram_a = gram_of(new_a)
    partial_a = lax.dot_general(new_a, tensor.reshape(NX, NY * NZ), (((0,), (0,)), ((), ())), precision=exact_mode, preferred_element_type=jnp.float32)
    partial_a = partial_a.reshape(RANK, NY, NZ)
    mttkrp_b = jnp.einsum("rjk,kr->jr", partial_a, factor_c, precision=exact_mode, preferred_element_type=jnp.float32)
    new_b = update_factor(factor_b, mttkrp_b, gram_a * gram_c)
    gram_bn = gram_of(new_b)
    mttkrp_c = jnp.einsum("rjk,jr->kr", partial_a, new_b, precision=exact_mode, preferred_element_type=jnp.float32)
    new_c = update_factor(factor_c, mttkrp_c, gram_a * gram_bn)
    return (new_a, new_b, new_c)
```

```python
import functools

import jax
import jax.numpy as jnp
from jax import lax
from jax.experimental import pallas as pl
from jax.experimental.pallas import tpu as pltpu
from jax.sharding import PartitionSpec as P

PASSES = 2
F32 = jnp.float32
BF16 = jnp.bfloat16
EXACT = lax.Precision.HIGHEST
ROWS = 128
RANK = 256
CHUNKS = 8
SUB = 16


def split(x):
    hi = x.astype(BF16)
    return hi, (x - hi.astype(F32)).astype(BF16)


def stream(x):
    hi, lo = split(x)
    return jnp.concatenate([hi, lo, hi], axis=1)


def weights(x):
    hi, lo = split(x)
    return jnp.concatenate([hi, hi, lo], axis=0)


def gram_of(factor):
    return lax.dot_general(
        factor, factor, (((0,), (0,)), ((), ())), precision=EXACT, preferred_element_type=F32
    )


def updated(factor, mttkrp, mix):
    scale = jnp.sum(mix, axis=0, keepdims=True) + 1.0
    for _ in range(PASSES):
        product = jnp.dot(factor, mix, precision=EXACT, preferred_element_type=F32)
        factor = jnp.maximum(factor + (mttkrp - product) / scale, 0.0)
    return factor


def put_mttkrp(buf, value):
    buf[0:128, :] = value[:, 0:128]
    buf[128:256, :] = value[:, 128:256]


def get_mttkrp(buf):
    return jnp.concatenate([buf[0:128, :], buf[128:256, :]], axis=1)


def put_half(buf, at, gram):
    buf[at : at + 128, :] = gram[0:128, 0:128]
    buf[at + 128 : at + 256, :] = gram[0:128, 128:256]
    buf[at + 256 : at + 384, :] = gram[128:256, 128:256]


def get_half(buf, at):
    corner = buf[at + 128 : at + 256, :]
    top = jnp.concatenate([buf[at : at + 128, :], corner], axis=1)
    low = jnp.concatenate([corner.T, buf[at + 256 : at + 384, :]], axis=1)
    return jnp.concatenate([top, low], axis=0)


def put_gram(buf, gram):
    buf[256:512, :] = gram[:, 0:128]
    buf[512:768, :] = gram[:, 128:256]


def get_gram(buf):
    return jnp.concatenate([buf[256:512, :], buf[512:768, :]], axis=1)


def fetch(tensor, held, sems):
    step = ROWS // CHUNKS
    copies = []
    for c in range(CHUNKS):
        part = pl.ds(c * step, step)
        copies.append(pltpu.make_async_copy(tensor.at[part], held.at[part], sems.at[c]))
    for copy in copies:
        copy.start()
    return copies


def first_kernel(inv_b, inv_c, tensor, fb, fc, out, held, sems):
    copies = fetch(tensor, held, sems)
    b, c = fb[...], fc[...]
    put_half(out, 256, gram_of(b) * inv_b)
    put_half(out, 640, gram_of(c) * inv_c)
    wide = weights(c)
    for n in range(ROWS // SUB):
        if n * SUB % (ROWS // CHUNKS) == 0:
            copies[n * SUB // (ROWS // CHUNKS)].wait()
        block = held[n * SUB : (n + 1) * SUB].reshape(SUB * 128, 128)
        prod = jnp.dot(stream(block), wide, preferred_element_type=F32)
        part = jnp.sum(prod.reshape(SUB, 128, RANK) * b[None], axis=1)
        out[n * SUB : (n + 1) * SUB, :] = part[:, 0:128]
        out[128 + n * SUB : 128 + (n + 1) * SUB, :] = part[:, 128:256]


def sum_over_x(copies, held, wide, a, turned, acc):
    acc[...] = jnp.zeros((128, RANK), F32)
    for n in range(ROWS // SUB):
        if n * SUB % (ROWS // CHUNKS) == 0:
            copies[n * SUB // (ROWS // CHUNKS)].wait()
        block = held[n * SUB : (n + 1) * SUB]
        if turned:
            block = jnp.swapaxes(block, 1, 2)
        prod = jnp.dot(
            stream(block.reshape(SUB * 128, 128)), wide, preferred_element_type=F32
        ).reshape(SUB, 128, RANK)
        total = acc[...]
        for i in range(SUB):
            row = n * SUB + i
            total = total + prod[i] * a[row : row + 1, :]
        acc[...] = total


def second_kernel(inv, tensor, red1, fa, fc, new_a, out, held, acc, sems):
    copies = fetch(tensor, held, sems)
    mix = get_half(red1, 256) * get_half(red1, 640)
    a = updated(fa[...], get_mttkrp(red1), mix)
    new_a[...] = a
    put_gram(out, gram_of(a) * inv)
    sum_over_x(copies, held, weights(fc[...]), a, False, acc)
    put_mttkrp(out, acc[...])


def third_kernel(inv, tensor, red1, red2, fa, fb, new_b, out, held, acc, sems):
    copies = fetch(tensor, held, sems)
    mix = get_gram(red2) * get_half(red1, 640)
    b = updated(fb[...], get_mttkrp(red2), mix)
    new_b[...] = b
    put_gram(out, gram_of(b) * inv)
    sum_over_x(copies, held, weights(b), fa[...], True, acc)
    put_mttkrp(out, acc[...])


def fourth_kernel(red2, red3, fc, new_c):
    mix = get_gram(red2) * get_gram(red3)
    new_c[...] = updated(fc[...], get_mttkrp(red3), mix)


VMEM_SPEC = pl.BlockSpec(memory_space=pltpu.VMEM)
ANY_SPEC = pl.BlockSpec(memory_space=pl.ANY)
HELD = pltpu.VMEM((ROWS, 128, 128), F32)
ACC = pltpu.VMEM((128, RANK), F32)
SEMS = pltpu.SemaphoreType.DMA((CHUNKS,))
FACTOR = jax.ShapeDtypeStruct((128, RANK), F32)


def buffer(rows):
    return jax.ShapeDtypeStruct((rows, 128), F32)


def kernel_call(body, name, n_in, outs, scratch):
    return pl.pallas_call(
        body,
        out_shape=outs,
        in_specs=([ANY_SPEC] if scratch else []) + [VMEM_SPEC] * n_in,
        out_specs=jax.tree.map(lambda _: VMEM_SPEC, outs),
        scratch_shapes=scratch,
        compiler_params=pltpu.CompilerParams(vmem_limit_bytes=56 * 2**20),
        name=name,
    )


def all_reduce(buf, axes, n):
    parts = buf.reshape(n, buf.shape[0] // n, 128)
    got = lax.all_to_all(parts, axes, 0, 0, tiled=True)
    mine = jnp.sum(got, axis=0)
    full = lax.all_to_all(jnp.broadcast_to(mine, parts.shape), axes, 0, 0, tiled=True)
    return full.reshape(buf.shape)


def per_device(sizes, tensor, factor_a, factor_b, factor_c):
    px, py, mz = sizes
    buf1 = kernel_call(
        functools.partial(first_kernel, 1.0 / mz, 1.0 / py), "mttkrp_a", 2, buffer(1024), [HELD, SEMS]
    )(tensor, factor_b, factor_c)
    red1 = all_reduce(buf1, ("py", "mz"), py * mz)
    new_a, buf2 = kernel_call(
        functools.partial(second_kernel, 1.0 / mz), "mttkrp_b", 3, [FACTOR, buffer(768)], [HELD, ACC, SEMS]
    )(tensor, red1, factor_a, factor_c)
    red2 = all_reduce(buf2, ("px", "mz"), px * mz)
    new_b, buf3 = kernel_call(
        functools.partial(third_kernel, 1.0 / px), "mttkrp_c", 4, [FACTOR, buffer(768)], [HELD, ACC, SEMS]
    )(tensor, red1, red2, new_a, factor_b)
    red3 = all_reduce(buf3, ("px", "py"), px * py)
    new_c = kernel_call(fourth_kernel, "update_c", 3, FACTOR, [])(red2, red3, factor_c)
    return (new_a, new_b, new_c)


def solution(mesh):
    sizes = tuple(mesh.shape[a] for a in ("px", "py", "mz"))
    in_specs = (P("px", "py", "mz"), P("px", None), P("py", None), P("mz", None))
    out_specs = (P("px", None), P("py", None), P("mz", None))
    return jax.shard_map(
        functools.partial(per_device, sizes),
        mesh=mesh,
        in_specs=in_specs,
        out_specs=out_specs,
        check_vma=False,
    )
```

```python
import functools

import jax
import jax.numpy as jnp
from jax import lax
from jax.experimental import pallas as pl
from jax.experimental.pallas import tpu as pltpu
from jax.sharding import PartitionSpec as P

PASSES = 2
F32 = jnp.float32
BF16 = jnp.bfloat16
EXACT = lax.Precision.HIGHEST
ROWS = 128
RANK = 256
CHUNKS = 4
SUB = 16


def split(x):
    hi = x.astype(BF16)
    return hi, (x - hi.astype(F32)).astype(BF16)


def stream(x):
    hi, lo = split(x)
    return jnp.concatenate([hi, lo, hi], axis=1)


def weights(x):
    hi, lo = split(x)
    return jnp.concatenate([hi, hi, lo], axis=0)


def gram_of(factor):
    hi, lo = split(factor)
    return lax.dot_general(
        jnp.concatenate([hi, lo, hi], axis=0),
        jnp.concatenate([hi, hi, lo], axis=0),
        (((0,), (0,)), ((), ())),
        preferred_element_type=F32,
    )


def updated(factor, mttkrp, mix):
    scale = jnp.sum(mix, axis=0, keepdims=True) + 1.0
    wide = weights(mix)
    for _ in range(PASSES):
        product = jnp.dot(stream(factor), wide, preferred_element_type=F32)
        factor = jnp.maximum(factor + (mttkrp - product) / scale, 0.0)
    return factor


def put_mttkrp(buf, value):
    buf[0:128, :] = value[:, 0:128]
    buf[128:256, :] = value[:, 128:256]


def get_mttkrp(buf):
    return jnp.concatenate([buf[0:128, :], buf[128:256, :]], axis=1)


def put_half(buf, at, gram):
    buf[at : at + 128, :] = gram[0:128, 0:128]
    buf[at + 128 : at + 256, :] = gram[0:128, 128:256]
    buf[at + 256 : at + 384, :] = gram[128:256, 128:256]


def get_half(buf, at):
    corner = buf[at + 128 : at + 256, :]
    top = jnp.concatenate([buf[at : at + 128, :], corner], axis=1)
    low = jnp.concatenate([corner.T, buf[at + 256 : at + 384, :]], axis=1)
    return jnp.concatenate([top, low], axis=0)


def put_gram(buf, gram):
    buf[256:512, :] = gram[:, 0:128]
    buf[512:768, :] = gram[:, 128:256]


def get_gram(buf):
    return jnp.concatenate([buf[256:512, :], buf[512:768, :]], axis=1)


def fetch(tensor, held, sems):
    step = ROWS // CHUNKS
    copies = []
    for c in range(CHUNKS):
        part = pl.ds(c * step, step)
        copies.append(pltpu.make_async_copy(tensor.at[part], held.at[part], sems.at[c]))
    copies[0].start()
    copies[1].start()
    return copies


def first_kernel(inv_b, inv_c, tensor, fb, fc, out, held, sems):
    copies = fetch(tensor, held, sems)
    b, c = fb[...], fc[...]
    put_half(out, 256, gram_of(b) * inv_b)
    put_half(out, 640, gram_of(c) * inv_c)
    wide = weights(c)
    for n in range(ROWS // SUB):
        if n * SUB % (ROWS // CHUNKS) == 0:
            at = n * SUB // (ROWS // CHUNKS)
            copies[at].wait()
            if at + 2 < CHUNKS:
                copies[at + 2].start()
        block = held[n * SUB : (n + 1) * SUB].reshape(SUB * 128, 128)
        prod = jnp.dot(stream(block), wide, preferred_element_type=F32)
        part = jnp.sum(prod.reshape(SUB, 128, RANK) * b[None], axis=1)
        out[n * SUB : (n + 1) * SUB, :] = part[:, 0:128]
        out[128 + n * SUB : 128 + (n + 1) * SUB, :] = part[:, 128:256]


def sum_over_x(copies, held, wide, a, turned, acc):
    acc[...] = jnp.zeros((128, RANK), F32)
    for n in range(ROWS // SUB):
        if n * SUB % (ROWS // CHUNKS) == 0:
            at = n * SUB // (ROWS // CHUNKS)
            copies[at].wait()
            if at + 2 < CHUNKS:
                copies[at + 2].start()
        block = held[n * SUB : (n + 1) * SUB]
        if turned:
            block = jnp.swapaxes(block, 1, 2)
        prod = jnp.dot(
            stream(block.reshape(SUB * 128, 128)), wide, preferred_element_type=F32
        ).reshape(SUB, 128, RANK)
        total = acc[...]
        for i in range(SUB):
            row = n * SUB + i
            total = total + prod[i] * a[row : row + 1, :]
        acc[...] = total


def second_kernel(inv, tensor, red1, fa, fc, new_a, out, held, acc, sems):
    copies = fetch(tensor, held, sems)
    mix = get_half(red1, 256) * get_half(red1, 640)
    a = updated(fa[...], get_mttkrp(red1), mix)
    new_a[...] = a
    put_gram(out, gram_of(a) * inv)
    sum_over_x(copies, held, weights(fc[...]), a, False, acc)
    put_mttkrp(out, acc[...])


def third_kernel(inv, tensor, red1, red2, fa, fb, new_b, out, held, acc, sems):
    copies = fetch(tensor, held, sems)
    mix = get_gram(red2) * get_half(red1, 640)
    b = updated(fb[...], get_mttkrp(red2), mix)
    new_b[...] = b
    put_gram(out, gram_of(b) * inv)
    sum_over_x(copies, held, weights(b), fa[...], True, acc)
    put_mttkrp(out, acc[...])


def fourth_kernel(red2, red3, fc, new_c):
    mix = get_gram(red2) * get_gram(red3)
    new_c[...] = updated(fc[...], get_mttkrp(red3), mix)


VMEM_SPEC = pl.BlockSpec(memory_space=pltpu.VMEM)
ANY_SPEC = pl.BlockSpec(memory_space=pltpu.HBM)
HELD = pltpu.VMEM((ROWS, 128, 128), F32)
ACC = pltpu.VMEM((128, RANK), F32)
SEMS = pltpu.SemaphoreType.DMA((CHUNKS,))
FACTOR = jax.ShapeDtypeStruct((128, RANK), F32)


def buffer(rows):
    return jax.ShapeDtypeStruct((rows, 128), F32)


def kernel_call(body, name, n_in, outs, scratch):
    return pl.pallas_call(
        body,
        out_shape=outs,
        in_specs=([ANY_SPEC] if scratch else []) + [VMEM_SPEC] * n_in,
        out_specs=jax.tree.map(lambda _: VMEM_SPEC, outs),
        scratch_shapes=scratch,
        compiler_params=pltpu.CompilerParams(vmem_limit_bytes=48 * 2**20),
        name=name,
    )


def all_reduce(buf, axes, n):
    parts = buf.reshape(n, buf.shape[0] // n, 128)
    got = lax.all_to_all(parts, axes, 0, 0, tiled=True)
    mine = jnp.sum(got, axis=0)
    full = lax.all_to_all(jnp.broadcast_to(mine, parts.shape), axes, 0, 0, tiled=True)
    return full.reshape(buf.shape)


def per_device(sizes, tensor, factor_a, factor_b, factor_c):
    px, py, mz = sizes
    buf1 = kernel_call(
        functools.partial(first_kernel, 1.0 / mz, 1.0 / py), "mttkrp_a", 2, buffer(1024), [HELD, SEMS]
    )(tensor, factor_b, factor_c)
    red1 = all_reduce(buf1, ("py", "mz"), py * mz)
    new_a, buf2 = kernel_call(
        functools.partial(second_kernel, 1.0 / mz), "mttkrp_b", 3, [FACTOR, buffer(768)], [HELD, ACC, SEMS]
    )(tensor, red1, factor_a, factor_c)
    red2 = all_reduce(buf2, ("px", "mz"), px * mz)
    new_b, buf3 = kernel_call(
        functools.partial(third_kernel, 1.0 / px), "mttkrp_c", 4, [FACTOR, buffer(768)], [HELD, ACC, SEMS]
    )(tensor, red1, red2, new_a, factor_b)
    red3 = all_reduce(buf3, ("px", "py"), px * py)
    new_c = kernel_call(fourth_kernel, "update_c", 3, FACTOR, [])(red2, red3, factor_c)
    return (new_a, new_b, new_c)


def solution(mesh):
    sizes = tuple(mesh.shape[a] for a in ("px", "py", "mz"))
    in_specs = (P("px", "py", "mz"), P("px", None), P("py", None), P("mz", None))
    out_specs = (P("px", None), P("py", None), P("mz", None))
    return jax.shard_map(
        functools.partial(per_device, sizes),
        mesh=mesh,
        in_specs=in_specs,
        out_specs=out_specs,
        check_vma=False,
    )
```

```python
import functools

import jax
import jax.numpy as jnp
from jax import lax
from jax.experimental import pallas as pl
from jax.experimental.pallas import tpu as pltpu
from jax.sharding import Mesh
from jax.sharding import PartitionSpec as P

PASSES = 2
F32 = jnp.float32
BF16 = jnp.bfloat16
EXACT = lax.Precision.HIGHEST
ROWS = 128
RANK = 256
CHUNKS = 4
SUB = 16


def split(x):
    hi = x.astype(BF16)
    return hi, (x - hi.astype(F32)).astype(BF16)


def stream(x):
    hi, lo = split(x)
    return jnp.concatenate([hi, lo, hi], axis=1)


def weights(x):
    hi, lo = split(x)
    return jnp.concatenate([hi, hi, lo], axis=0)


def gram_of(factor):
    hi, lo = split(factor)
    return lax.dot_general(
        jnp.concatenate([hi, lo, hi], axis=0),
        jnp.concatenate([hi, hi, lo], axis=0),
        (((0,), (0,)), ((), ())),
        preferred_element_type=F32,
    )


def updated(factor, mttkrp, mix):
    scale = jnp.sum(mix, axis=0, keepdims=True) + 1.0
    wide = weights(mix)
    for _ in range(PASSES):
        product = jnp.dot(stream(factor), wide, preferred_element_type=F32)
        factor = jnp.maximum(factor + (mttkrp - product) / scale, 0.0)
    return factor


def put_mttkrp(buf, value):
    buf[0:128, :] = value[:, 0:128]
    buf[128:256, :] = value[:, 128:256]


def get_mttkrp(buf):
    return jnp.concatenate([buf[0:128, :], buf[128:256, :]], axis=1)


def put_half(out, core, at, gram):
    out[core, at : at + 128, :] = gram[0:128, 0:128]
    out[core, at + 128 : at + 192, :] = gram[0:64, 128:256]
    out[1 - core, at : at + 64, :] = gram[64:128, 128:256]
    out[1 - core, at + 64 : at + 192, :] = gram[128:256, 128:256]


def halves(a, b):
    first = lax.axis_index("core") == 0
    return jnp.where(first, a, b), jnp.where(first, b, a)


def get_rows(lo, hi):
    left = jnp.concatenate([lo[0:64], hi[0:64]], axis=0)
    right = jnp.concatenate([lo[64:128], hi[64:128]], axis=0)
    return jnp.concatenate([left, right], axis=1)


def get_half(lo, hi, at):
    corner = jnp.concatenate([lo[at + 128 : at + 192], hi[at : at + 64]], axis=0)
    top = jnp.concatenate([lo[at : at + 128], corner], axis=1)
    low = jnp.concatenate([corner.T, hi[at + 64 : at + 192]], axis=1)
    return jnp.concatenate([top, low], axis=0)


def put_gram(buf, gram):
    first = lax.axis_index("core") == 0
    buf[256:512, :] = jnp.where(first, gram[:, 0:128], gram[:, 128:256])


def get_gram(mine, other):
    return jnp.concatenate(halves(mine[256:512, :], other[...]), axis=1)


def fetch(tensor, held, sems):
    step = ROWS // CHUNKS
    copies = []
    for c in range(CHUNKS):
        part = pl.ds(c * step, step)
        copies.append(pltpu.make_async_copy(tensor.at[part], held.at[part], sems.at[c]))
    copies[0].start()
    copies[1].start()
    return copies


def first_kernel(inv_b, inv_c, tensor, fb, fc, out, held, sems):
    copies = fetch(tensor, held, sems)
    b, c = fb[...], fc[...]
    core = lax.axis_index("core")
    put_half(out, core, 128, gram_of(b) * inv_b)
    put_half(out, core, 320, gram_of(c) * inv_c)
    wide = weights(c)
    for n in range(ROWS // SUB):
        if n * SUB % (ROWS // CHUNKS) == 0:
            at = n * SUB // (ROWS // CHUNKS)
            copies[at].wait()
            if at + 2 < CHUNKS:
                copies[at + 2].start()
        block = held[n * SUB : (n + 1) * SUB].reshape(SUB * 128, 128)
        prod = jnp.dot(stream(block), wide, preferred_element_type=F32)
        part = jnp.sum(prod.reshape(SUB, 128, RANK) * b[None], axis=1)
        half, at = divmod(n * SUB, 64)
        slot = core if half == 0 else 1 - core
        out[slot, at : at + SUB, :] = part[:, 0:128]
        out[slot, 64 + at : 64 + at + SUB, :] = part[:, 128:256]


def sum_over_x(copies, held, wide, a, turned, acc):
    acc[...] = jnp.zeros((128, RANK), F32)
    for n in range(ROWS // SUB):
        if n * SUB % (ROWS // CHUNKS) == 0:
            at = n * SUB // (ROWS // CHUNKS)
            copies[at].wait()
            if at + 2 < CHUNKS:
                copies[at + 2].start()
        block = held[n * SUB : (n + 1) * SUB]
        if turned:
            block = jnp.swapaxes(block, 1, 2)
        prod = jnp.dot(
            stream(block.reshape(SUB * 128, 128)), wide, preferred_element_type=F32
        ).reshape(SUB, 128, RANK)
        total = acc[...]
        for i in range(SUB):
            row = n * SUB + i
            total = total + prod[i] * a[row : row + 1, :]
        acc[...] = total


def second_kernel(inv, tensor, mine1, other1, fa, fc, new_a, again, out, held, acc, sems):
    copies = fetch(tensor, held, sems)
    lo, hi = halves(mine1[...], other1[...])
    mix = get_half(lo, hi, 128) * get_half(lo, hi, 320)
    a = updated(fa[...], get_rows(lo, hi), mix)
    new_a[...] = a
    again[...] = a
    put_gram(out, gram_of(a) * inv)
    sum_over_x(copies, held, weights(fc[...]), a, False, acc)
    put_mttkrp(out, acc[...])


def third_kernel(inv, tensor, mine1, other1, red2, swap2, fa, fb, new_b, out, held, acc, sems):
    copies = fetch(tensor, held, sems)
    mix = get_gram(red2, swap2) * get_half(*halves(mine1[...], other1[...]), 320)
    b = updated(fb[...], get_mttkrp(red2), mix)
    new_b[...] = b
    core = lax.axis_index("core")
    put_half(out, core, 128, gram_of(b) * inv)
    sum_over_x(copies, held, weights(b), fa[...], True, acc)
    for half, slot in enumerate((core, 1 - core)):
        part = acc[half * 64 : half * 64 + 64, :]
        out[slot, 0:64, :] = part[:, 0:128]
        out[slot, 64:128, :] = part[:, 128:256]


def fourth_kernel(red2, swap2, mine3, other3, fc, new_c):
    lo, hi = halves(mine3[...], other3[...])
    mix = get_gram(red2, swap2) * get_half(lo, hi, 128)
    new_c[...] = updated(fc[...], get_rows(lo, hi), mix)


VMEM_SPEC = pl.BlockSpec(memory_space=pltpu.VMEM)
ANY_SPEC = pl.BlockSpec(memory_space=pltpu.HBM)
HELD = pltpu.VMEM((ROWS, 128, 128), F32)
ACC = pltpu.VMEM((128, RANK), F32)
SEMS = pltpu.SemaphoreType.DMA((CHUNKS,))
FACTOR = jax.ShapeDtypeStruct((128, RANK), F32)


def buffer(rows):
    return jax.ShapeDtypeStruct((rows, 128), F32)


def kernel_call(body, name, n_in, outs, scratch):
    return pl.pallas_call(
        body,
        out_shape=outs,
        in_specs=([ANY_SPEC] if scratch else []) + [VMEM_SPEC] * n_in,
        out_specs=jax.tree.map(lambda _: VMEM_SPEC, outs),
        scratch_shapes=scratch,
        compiler_params=pltpu.CompilerParams(vmem_limit_bytes=48 * 2**20),
        name=name,
    )


def all_reduce(buf, axes, n):
    parts = buf.reshape(n, buf.shape[0] // n, 128)
    got = lax.all_to_all(parts, axes, 0, 0, tiled=True)
    mine = jnp.sum(got, axis=0)
    full = lax.all_to_all(jnp.broadcast_to(mine, parts.shape), axes, 0, 0, tiled=True)
    return full.reshape(buf.shape)


def swap(x):
    return lax.ppermute(x, "core", [(0, 1), (1, 0)])


def core_first(buf, axes, n):
    mine = all_reduce(buf[0] + swap(buf[1]), axes, n)
    return mine, swap(mine)


def pair(rows):
    return jax.ShapeDtypeStruct((2, rows, 128), F32)


def per_device(sizes, tensor, factor_a, factor_b, factor_c):
    px, y, core, mz = sizes
    buf1 = kernel_call(
        functools.partial(first_kernel, 1.0 / mz, 1.0 / (y * core)), "mttkrp_a", 2, pair(512), [HELD, SEMS]
    )(tensor, factor_b, factor_c)
    mine1, other1 = core_first(buf1, ("y", "mz"), y * mz)
    new_a, held_a, buf2 = kernel_call(
        functools.partial(second_kernel, 1.0 / mz), "mttkrp_b", 4, [FACTOR, FACTOR, buffer(512)], [HELD, ACC, SEMS]
    )(tensor, mine1, other1, factor_a, factor_c)
    red2 = all_reduce(buf2, ("px", "mz"), px * mz)
    swap2 = swap(red2[256:512])
    new_b, buf3 = kernel_call(
        functools.partial(third_kernel, 1.0 / px), "mttkrp_c", 6, [FACTOR, pair(320)], [HELD, ACC, SEMS]
    )(tensor, mine1, other1, red2, swap2, held_a, factor_b)
    mine3, other3 = core_first(buf3, ("px", "y"), px * y)
    new_c = kernel_call(fourth_kernel, "update_c", 5, FACTOR, [])(red2, swap2, mine3, other3, factor_c)
    return (new_a, new_b, new_c)


def solution(mesh):
    px, py, mz = (mesh.shape[a] for a in ("px", "py", "mz"))
    sizes = (px, py // 2, 2, mz)
    fine = Mesh(mesh.devices.reshape(sizes), ("px", "y", "core", "mz"))
    by_y = P(("y", "core"), None)
    in_specs = (P("px", ("y", "core"), "mz"), P("px", None), by_y, P("mz", None))
    return jax.shard_map(
        functools.partial(per_device, sizes),
        mesh=fine,
        in_specs=in_specs,
        out_specs=(P("px", None), by_y, P("mz", None)),
        check_vma=False,
    )
```

```python
import functools

import jax
import jax.numpy as jnp
from jax import lax
from jax.experimental import pallas as pl
from jax.experimental.pallas import tpu as pltpu
from jax.sharding import Mesh
from jax.sharding import PartitionSpec as P

PASSES = 2
F32 = jnp.float32
BF16 = jnp.bfloat16
EXACT = lax.Precision.HIGHEST
ROWS = 128
RANK = 256
CHUNKS = 4
SUB = 16


def split(x):
    hi = x.astype(BF16)
    return hi, (x - hi.astype(F32)).astype(BF16)


def stream(x):
    hi, lo = split(x)
    return jnp.concatenate([hi, lo, hi], axis=1)


def weights(x):
    hi, lo = split(x)
    return jnp.concatenate([hi, hi, lo], axis=0)


def gram_of(factor):
    hi, lo = split(factor)
    return lax.dot_general(
        jnp.concatenate([hi, lo, hi], axis=0),
        jnp.concatenate([hi, hi, lo], axis=0),
        (((0,), (0,)), ((), ())),
        preferred_element_type=F32,
    )


def updated(factor, mttkrp, mix):
    scale = jnp.sum(mix, axis=0, keepdims=True) + 1.0
    wide = weights(mix)
    for _ in range(PASSES):
        product = jnp.dot(stream(factor), wide, preferred_element_type=F32)
        factor = jnp.maximum(factor + (mttkrp - product) / scale, 0.0)
    return factor


def put_mttkrp(buf, value):
    buf[0:128, :] = value[:, 0:128]
    buf[128:256, :] = value[:, 128:256]


def get_mttkrp(buf):
    return jnp.concatenate([buf[0:128, :], buf[128:256, :]], axis=1)


def put_half(out, core, at, gram):
    out[core, at : at + 128, :] = gram[0:128, 0:128]
    out[core, at + 128 : at + 192, :] = gram[0:64, 128:256]
    out[1 - core, at : at + 64, :] = gram[64:128, 128:256]
    out[1 - core, at + 64 : at + 192, :] = gram[128:256, 128:256]


def halves(a, b):
    first = lax.axis_index("core") == 0
    return jnp.where(first, a, b), jnp.where(first, b, a)


def get_rows(lo, hi):
    left = jnp.concatenate([lo[0:64], hi[0:64]], axis=0)
    right = jnp.concatenate([lo[64:128], hi[64:128]], axis=0)
    return jnp.concatenate([left, right], axis=1)


def get_half(lo, hi, at):
    corner = jnp.concatenate([lo[at + 128 : at + 192], hi[at : at + 64]], axis=0)
    top = jnp.concatenate([lo[at : at + 128], corner], axis=1)
    low = jnp.concatenate([corner.T, hi[at + 64 : at + 192]], axis=1)
    return jnp.concatenate([top, low], axis=0)


def put_gram(buf, gram):
    first = lax.axis_index("core") == 0
    lo = jnp.concatenate([gram[0:128, 0:128], gram[0:64, 128:256]], axis=0)
    hi = jnp.concatenate([gram[64:128, 128:256], gram[128:256, 128:256]], axis=0)
    buf[256:448, :] = jnp.where(first, lo, hi)


def get_gram(mine, other):
    return get_half(*halves(mine[256:448, :], other[...]), 0)


def fetch(tensor, held, sems):
    step = ROWS // CHUNKS
    copies = []
    for c in range(CHUNKS):
        part = pl.ds(c * step, step)
        copies.append(pltpu.make_async_copy(tensor.at[part], held.at[part], sems.at[c]))
    copies[0].start()
    copies[1].start()
    return copies


def first_kernel(inv_b, inv_c, tensor, fbc, out, held, sems):
    copies = fetch(tensor, held, sems)
    b, c = fbc[0], fbc[1]
    core = lax.axis_index("core")
    put_half(out, core, 128, gram_of(b) * inv_b)
    put_half(out, core, 320, gram_of(c) * inv_c)
    wide = weights(c)
    for n in range(ROWS // SUB):
        if n * SUB % (ROWS // CHUNKS) == 0:
            at = n * SUB // (ROWS // CHUNKS)
            copies[at].wait()
            if at + 2 < CHUNKS:
                copies[at + 2].start()
        block = held[n * SUB : (n + 1) * SUB].reshape(SUB * 128, 128)
        prod = jnp.dot(stream(block), wide, preferred_element_type=F32)
        part = jnp.sum(prod.reshape(SUB, 128, RANK) * b[None], axis=1)
        half, at = divmod(n * SUB, 64)
        slot = core if half == 0 else 1 - core
        out[slot, at : at + SUB, :] = part[:, 0:128]
        out[slot, 64 + at : 64 + at + SUB, :] = part[:, 128:256]


def sum_over_x(copies, held, wide, a, turned, acc):
    acc[...] = jnp.zeros((128, RANK), F32)
    for n in range(ROWS // SUB):
        if n * SUB % (ROWS // CHUNKS) == 0:
            at = n * SUB // (ROWS // CHUNKS)
            copies[at].wait()
            if at + 2 < CHUNKS:
                copies[at + 2].start()
        block = held[n * SUB : (n + 1) * SUB]
        if turned:
            block = jnp.swapaxes(block, 1, 2)
        prod = jnp.dot(
            stream(block.reshape(SUB * 128, 128)), wide, preferred_element_type=F32
        ).reshape(SUB, 128, RANK)
        total = acc[...]
        for i in range(SUB):
            row = n * SUB + i
            total = total + prod[i] * a[row : row + 1, :]
        acc[...] = total


def second_kernel(inv, tensor, mine1, other1, fa, fc, new_a, again, out, held, acc, sems):
    copies = fetch(tensor, held, sems)
    lo, hi = halves(mine1[...], other1[...])
    mix = get_half(lo, hi, 128) * get_half(lo, hi, 320)
    a = updated(fa[...], get_rows(lo, hi), mix)
    new_a[...] = a
    again[...] = a
    put_gram(out, gram_of(a) * inv)
    sum_over_x(copies, held, weights(fc[...]), a, False, acc)
    put_mttkrp(out, acc[...])


def third_kernel(inv, tensor, mine1, other1, red2, swap2, fa, fb, new_b, out, held, acc, sems):
    copies = fetch(tensor, held, sems)
    mix = get_gram(red2, swap2) * get_half(*halves(mine1[...], other1[...]), 320)
    b = updated(fb[...], get_mttkrp(red2), mix)
    new_b[...] = b
    core = lax.axis_index("core")
    put_half(out, core, 128, gram_of(b) * inv)
    sum_over_x(copies, held, weights(b), fa[...], True, acc)
    for half, slot in enumerate((core, 1 - core)):
        part = acc[half * 64 : half * 64 + 64, :]
        out[slot, 0:64, :] = part[:, 0:128]
        out[slot, 64:128, :] = part[:, 128:256]


def fourth_kernel(red2, swap2, mine3, other3, fc, new_c):
    lo, hi = halves(mine3[...], other3[...])
    mix = get_gram(red2, swap2) * get_half(lo, hi, 128)
    new_c[...] = updated(fc[...], get_rows(lo, hi), mix)


VMEM_SPEC = pl.BlockSpec(memory_space=pltpu.VMEM)
ANY_SPEC = pl.BlockSpec(memory_space=pltpu.HBM)
HELD = pltpu.VMEM((ROWS, 128, 128), F32)
ACC = pltpu.VMEM((128, RANK), F32)
SEMS = pltpu.SemaphoreType.DMA((CHUNKS,))
FACTOR = jax.ShapeDtypeStruct((128, RANK), F32)


def buffer(rows):
    return jax.ShapeDtypeStruct((rows, 128), F32)


def kernel_call(body, name, n_in, outs, scratch):
    return pl.pallas_call(
        body,
        out_shape=outs,
        in_specs=([ANY_SPEC] if scratch else []) + [VMEM_SPEC] * n_in,
        out_specs=jax.tree.map(lambda _: VMEM_SPEC, outs),
        scratch_shapes=scratch,
        compiler_params=pltpu.CompilerParams(vmem_limit_bytes=48 * 2**20),
        name=name,
    )


def all_reduce(buf, axes, n):
    parts = buf.reshape(n, buf.shape[0] // n, 128)
    got = lax.all_to_all(parts, axes, 0, 0, tiled=True)
    mine = jnp.sum(got, axis=0)
    full = lax.all_to_all(jnp.broadcast_to(mine, parts.shape), axes, 0, 0, tiled=True)
    return full.reshape(buf.shape)


def swap(x):
    return lax.ppermute(x, "core", [(0, 1), (1, 0)])


def core_first(buf, axes, n):
    mine = all_reduce(buf[0] + swap(buf[1]), axes, n)
    return mine, swap(mine)


def pair(rows):
    return jax.ShapeDtypeStruct((2, rows, 128), F32)


def per_device(sizes, tensor, factor_a, factor_b, factor_c):
    px, y, core, mz = sizes
    buf1 = kernel_call(
        functools.partial(first_kernel, 1.0 / mz, 1.0 / (y * core)), "mttkrp_a", 1, pair(512), [HELD, SEMS]
    )(tensor, jnp.stack([factor_b, factor_c]))
    mine1, other1 = core_first(buf1, ("y", "mz"), y * mz)
    new_a, held_a, buf2 = kernel_call(
        functools.partial(second_kernel, 1.0 / mz), "mttkrp_b", 4, [FACTOR, FACTOR, buffer(448)], [HELD, ACC, SEMS]
    )(tensor, mine1, other1, factor_a, factor_c)
    red2 = all_reduce(buf2, ("px", "mz"), px * mz)
    swap2 = swap(red2[256:448])
    new_b, buf3 = kernel_call(
        functools.partial(third_kernel, 1.0 / px), "mttkrp_c", 6, [FACTOR, pair(320)], [HELD, ACC, SEMS]
    )(tensor, mine1, other1, red2, swap2, held_a, factor_b)
    mine3, other3 = core_first(buf3, ("px", "y"), px * y)
    new_c = kernel_call(fourth_kernel, "update_c", 5, FACTOR, [])(red2, swap2, mine3, other3, factor_c)
    return (new_a, new_b, new_c)


def solution(mesh):
    px, py, mz = (mesh.shape[a] for a in ("px", "py", "mz"))
    sizes = (px, py // 2, 2, mz)
    fine = Mesh(mesh.devices.reshape(sizes), ("px", "y", "core", "mz"))
    by_y = P(("y", "core"), None)
    in_specs = (P("px", ("y", "core"), "mz"), P("px", None), by_y, P("mz", None))
    return jax.shard_map(
        functools.partial(per_device, sizes),
        mesh=fine,
        in_specs=in_specs,
        out_specs=(P("px", None), by_y, P("mz", None)),
        check_vma=False,
    )
```
